32 devices in a mesh: ctx: 8 (over z, core), head: 4 (over y, x).
Axes of the slice: x: 2, y: 2, z: 4, core: 2. Of those that a mesh axis runs over, the one named last changes fastest.
Arguments:
- queries: bfloat16 [12288, 3072], P('ctx', 'head'), may hold values from -160 to 160
- key_states: bfloat16 [12288, 3072], P('ctx', 'head'), may hold values from -12 to 12
- value_states: bfloat16 [12288, 3072], P('ctx', 'head'), may hold values from -18 to 18
- out_grads: bfloat16 [12288, 3072], P(('ctx', 'head')), may hold values from -6 to 6
- pattern: int32 [32, 8], replicated, may hold values from -1 to 31, as said below
Outputs:
- attended: bfloat16 [12288, 3072], P(('ctx', 'head'))
- query_grads: bfloat16 [12288, 3072], P('ctx', 'head')
- key_grads: bfloat16 [12288, 3072], P('ctx', 'head')
- value_grads: bfloat16 [12288, 3072], P('ctx', 'head')
The draws below stay inside these ranges and needn't reach their ends.
Inputs may be any that keep to these rules, and one draw needn't show every extreme that they name: `pattern`: row t lists distinct tiles whose frame tile (tile // 4) differs from that of t by at most one; t itself is always listed; -1 marks an empty slot and empty slots come last; three or more tiles are listed in every row.
All inputs are finite; a program needn't handle non-finite values.
Results may differ from the reference program's by a relative error of at most 0.035.
Values may be sent and summed in bfloat16 or wider, within the bound.
A program may use at most 320 MiB of HBM per device.

```python
import math
import jax
import jax.numpy as jnp
from jax import lax

HEADS = 24
HD = 128
D = 3072
TILE = 384
SPT = 4
KSLOT = 8
TOKENS = 12288
TILES = 32


def shared_base(key):
    noise_q = jnp.clip(jax.random.normal(jax.random.fold_in(key, 11), (TOKENS, D), jnp.float32), -6.0, 6.0)
    noise_k = jnp.clip(jax.random.normal(jax.random.fold_in(key, 12), (TOKENS, D), jnp.float32), -6.0, 6.0)
    return (noise_q, noise_k)


def draw_queries(key, part):
    noise_q, noise_k = shared_base(key)
    result = noise_q
    return jnp.clip(result, -160.0, 160.0).astype(jnp.bfloat16)


def draw_key_states(key, part):
    noise_q, noise_k = shared_base(key)
    result = noise_k
    return jnp.clip(result, -12.0, 12.0).astype(jnp.bfloat16)


def draw_value_states(key, part):
    noise = jnp.clip(jax.random.normal(jax.random.fold_in(key, 21), (TOKENS, D), jnp.float32), -6.0, 6.0)
    return jnp.clip(noise, -18.0, 18.0).astype(jnp.bfloat16)


def draw_pattern(key, part):
    frame_tiles = TILES // SPT
    own_ids = jnp.arange(TILES, dtype=jnp.int32)
    frame_ids = own_ids // SPT
    offsets = jnp.arange(3 * SPT, dtype=jnp.int32)
    cand_frame = frame_ids[:, None] + offsets[None, :] // SPT - 1
    candidates = cand_frame * SPT + offsets[None, :] % SPT
    inside = (cand_frame >= 0) & (cand_frame < frame_tiles)
    ranking = jax.random.randint(jax.random.fold_in(key, 31), (TILES, 3 * SPT), 0, 1 << 20, jnp.int32) * (4 * SPT) + offsets[None, :]
    ranking = jnp.where(candidates == own_ids[:, None], -1, ranking)
    ranking = jnp.where(inside, ranking, 1 << 30)
    ordering = jnp.argsort(ranking, axis=1)
    picked = jnp.take_along_axis(candidates, ordering, axis=1)[:, :KSLOT]
    counts = jax.random.randint(jax.random.fold_in(key, 32), (TILES,), 3, KSLOT + 1, jnp.int32)
    counts = counts.at[0].set(KSLOT)
    slot_ids = jnp.arange(KSLOT, dtype=jnp.int32)
    return jnp.where(slot_ids[None, :] < counts[:, None], picked, -1).astype(jnp.int32)


def levels(key, shape, pieces, smallest, largest):
    level, own = 1.0, jax.random.fold_in(key, 6)
    for axis_at, parts in pieces:
        steps = jnp.exp(jax.random.uniform(jax.random.fold_in(own, axis_at), (parts,), jnp.float32, smallest / len(pieces), largest / len(pieces)))
        level = level * jnp.repeat(steps, shape[axis_at] // parts).reshape([-1 if axis == axis_at else 1 for axis in range(len(shape))])
    return level


def scatter_about(key, extent, scale, limit, shards=(), held_as=jnp.bfloat16):
    drawn = scale * jax.random.normal(key, extent, jnp.float32)
    if shards:
        drawn = drawn * levels(key, extent, shards, -0.22, 0.18)
    return jnp.clip(drawn, -limit, limit).astype(held_as)


def setup_inputs(seed: int = 0) -> dict:
    streams_of = jax.random.split(jax.random.key(seed), 6)
    return {
        "queries": draw_queries(jax.random.fold_in(streams_of[5], 71), 0),
        "key_states": draw_key_states(jax.random.fold_in(streams_of[5], 71), 0),
        "value_states": draw_value_states(jax.random.fold_in(streams_of[5], 71), 0),
        "out_grads": scatter_about(streams_of[3], (TOKENS, D), 1.0, 6.0, ((0, 32),)),
        "pattern": draw_pattern(jax.random.fold_in(streams_of[5], 71), 0),
    }


def slot_lookup(pattern, tile_num):
    listed = pattern[tile_num]
    allowed = listed >= 0
    safe_slots = jnp.where(allowed, listed, tile_num).astype(jnp.int32)
    return (allowed, safe_slots)

def tile_scores(query_tile, key_sel, allowed):
    score_scale = 1.0 / math.sqrt(HD)
    scores = jnp.einsum('qhd,sthd->hqst', query_tile.astype(jnp.float32), key_sel.astype(jnp.float32)) * score_scale
    return jnp.where(allowed[None, None, :, None], scores, -jnp.inf)

def reference(queries, key_states, value_states, out_grads, pattern):
    score_scale = 1.0 / math.sqrt(HD)
    query_tiles = queries.reshape(TILES, TILE, HEADS, HD)
    key_tiles = key_states.reshape(TILES, TILE, HEADS, HD)
    value_tiles = value_states.reshape(TILES, TILE, HEADS, HD)
    grad_tiles = out_grads.reshape(TILES, TILE, HEADS, HD)

    def forward_tile(tile_num):
        allowed, safe_slots = slot_lookup(pattern, tile_num)
        key_sel = key_tiles[safe_slots]
        value_sel = value_tiles[safe_slots]
        scores = tile_scores(query_tiles[tile_num], key_sel, allowed)
        row_max = lax.optimization_barrier(jnp.max(scores, axis=(2, 3)))
        row_total = lax.optimization_barrier(jnp.sum(jnp.exp(scores - row_max[:, :, None, None]), axis=(2, 3)))
        log_total = row_max + jnp.log(row_total)
        weights = jnp.exp(scores - log_total[:, :, None, None]).astype(jnp.bfloat16)
        result = jnp.einsum('hqst,sthd->qhd', weights.astype(jnp.float32), value_sel.astype(jnp.float32))
        return (result.astype(jnp.bfloat16), log_total)
    tile_ids = jnp.arange(TILES, dtype=jnp.int32)
    attended, log_totals = lax.map(forward_tile, tile_ids)
    delta = lax.optimization_barrier(jnp.sum(grad_tiles.astype(jnp.float32) * attended.astype(jnp.float32), axis=-1))

    def backward_tile(grad_sums, tile_num):
        allowed, safe_slots = slot_lookup(pattern, tile_num)
        key_sel = key_tiles[safe_slots]
        value_sel = value_tiles[safe_slots]
        query_tile = query_tiles[tile_num].astype(jnp.float32)
        grad_tile = grad_tiles[tile_num].astype(jnp.float32)
        scores = tile_scores(query_tiles[tile_num], key_sel, allowed)
        weights = jnp.exp(scores - log_totals[tile_num][:, :, None, None])
        weights_low = weights.astype(jnp.bfloat16)
        grad_weights = jnp.einsum('qhd,sthd->hqst', grad_tile, value_sel.astype(jnp.float32))
        delta_tile = jnp.transpose(delta[tile_num])
        grad_scores = (weights * (grad_weights - delta_tile[:, :, None, None])).astype(jnp.bfloat16)
        query_grad = jnp.einsum('hqst,sthd->qhd', grad_scores.astype(jnp.float32), key_sel.astype(jnp.float32)) * score_scale
        key_terms = jnp.einsum('hqst,qhd->sthd', grad_scores.astype(jnp.float32), query_tile) * score_scale
        value_terms = jnp.einsum('hqst,qhd->sthd', weights_low.astype(jnp.float32), grad_tile)
        keep = allowed[:, None, None, None]
        key_sums = grad_sums[0].at[safe_slots].add(jnp.where(keep, key_terms, 0.0))
        value_sums = grad_sums[1].at[safe_slots].add(jnp.where(keep, value_terms, 0.0))
        return ((key_sums, value_sums), query_grad.astype(jnp.bfloat16))
    zero_grads = jnp.zeros((TILES, TILE, HEADS, HD), jnp.float32)
    (key_sums, value_sums), query_grads = lax.scan(backward_tile, (zero_grads, zero_grads), tile_ids)
    return (attended.reshape(TOKENS, D), query_grads.reshape(TOKENS, D), key_sums.astype(jnp.bfloat16).reshape(TOKENS, D), value_sums.astype(jnp.bfloat16).reshape(TOKENS, D))
```

```python
import functools
import math

import jax
import jax.numpy as jnp
from jax import lax
from jax.experimental import pallas as pl
from jax.experimental.pallas import tpu as pltpu
from jax.sharding import PartitionSpec as P

HD = 128
TILE = 384
SPT = 4
KSLOT = 8
SCALE = 1.0 / math.sqrt(HD)
EXP2_SCALE = SCALE * math.log2(math.e)


def dot_nn(a, b):
    return lax.dot_general(a, b, (((1,), (0,)), ((), ())), preferred_element_type=jnp.float32)


def dot_nt(a, b):
    return lax.dot_general(a, b, (((1,), (1,)), ((), ())), preferred_element_type=jnp.float32)


def fold_rows(block, op):
    return op(block.reshape(TILE // 8, 8, TILE), axis=0)


def attention_kernel(
    heads, own_tiles, first_col,
    idx_ref, cnt_ref, q_ref, do_ref, k_hbm, v_hbm, low_hbm, high_hbm,
    o_ref, dq_ref, dk_own, dv_own, low_out, high_out,
    kext, vext, kt, vt, scores, dk, dv, o_acc, dq_acc, sems,
):
    a = pl.program_id(0)
    ext_tiles = own_tiles + 2 * SPT
    width = heads * HD
    cols = [slice(h * HD, (h + 1) * HD) for h in range(heads)]

    @pl.when(a == 0)
    def _():
        copies = []
        for n, (dst, own_src, part) in enumerate(((kext, k_hbm, 0), (vext, v_hbm, 1))):
            rim = pl.ds(part * width, width)
            copies.append(pltpu.make_async_copy(
                low_hbm.at[:, :, rim], dst.at[pl.ds(0, SPT)], sems.at[3 * n]))
            copies.append(pltpu.make_async_copy(
                own_src.at[:, :, pl.ds(first_col, width)], dst.at[pl.ds(SPT, own_tiles)],
                sems.at[3 * n + 1]))
            copies.append(pltpu.make_async_copy(
                high_hbm.at[:, :, rim], dst.at[pl.ds(SPT + own_tiles, SPT)], sems.at[3 * n + 2]))
        for copy in copies:
            copy.start()
        dk[...] = jnp.zeros_like(dk)
        dv[...] = jnp.zeros_like(dv)
        for copy in copies:
            copy.wait()

        @pl.loop(0, ext_tiles)
        def _(t):
            for h in range(heads):
                kt[h, t] = kext[t, :, cols[h]].T
                vt[h, t] = vext[t, :, cols[h]].T

    count = cnt_ref[a]

    def score_slot(s, tops):
        t = idx_ref[a * KSLOT + s]
        new = []
        for h in range(heads):
            block = dot_nt(kext[t, :, cols[h]], q_ref[:, cols[h]])
            scores[h, s] = block
            new.append(jnp.maximum(tops[h], fold_rows(block, jnp.max)))
        return tuple(new)

    tops = lax.fori_loop(
        0, count, score_slot, tuple(jnp.full((8, TILE), -jnp.inf, jnp.float32) for _ in cols)
    )
    tops = [jnp.max(top, axis=0, keepdims=True) for top in tops]

    def exp_slot(s, sums):
        new = []
        for h in range(heads):
            block = jnp.exp2((scores[h, s] - tops[h]) * EXP2_SCALE)
            scores[h, s] = block
            new.append(sums[h] + fold_rows(block, jnp.sum))
        return tuple(new)

    sums = lax.fori_loop(
        0, count, exp_slot, tuple(jnp.zeros((8, TILE), jnp.float32) for _ in cols)
    )
    inverse = [1.0 / jnp.sum(total, axis=0, keepdims=True) for total in sums]

    o_acc[...] = jnp.zeros_like(o_acc)
    dq_acc[...] = jnp.zeros_like(dq_acc)

    @pl.loop(0, count)
    def _(s):
        t = idx_ref[a * KSLOT + s]
        for h in range(heads):
            weights = scores[h, s] * inverse[h]
            scores[h, s] = weights
            low = weights.astype(jnp.bfloat16)
            o_acc[h] += dot_nn(vt[h, t], low)
            dv[t, :, cols[h]] += dot_nn(low, do_ref[:, cols[h]])

    deltas = []
    for h in range(heads):
        out_t = o_acc[h].astype(jnp.bfloat16).astype(jnp.float32)
        grads_t = do_ref[:, cols[h]].astype(jnp.float32).T
        deltas.append(jnp.sum(out_t * grads_t, axis=0, keepdims=True))
        o_ref[:, cols[h]] = out_t.T.astype(jnp.bfloat16)

    @pl.loop(0, count)
    def _(s):
        t = idx_ref[a * KSLOT + s]
        for h in range(heads):
            grads = dot_nt(vext[t, :, cols[h]], do_ref[:, cols[h]])
            low = (scores[h, s] * (grads - deltas[h])).astype(jnp.bfloat16)
            dk[t, :, cols[h]] += dot_nn(low, q_ref[:, cols[h]])
            dq_acc[h] += dot_nn(kt[h, t], low)

    for h in range(heads):
        dq_ref[:, cols[h]] = (dq_acc[h] * SCALE).T.astype(jnp.bfloat16)

    @pl.when(a == own_tiles - 1)
    def _():
        own = pl.ds(SPT, own_tiles)

        @pl.loop(0, ext_tiles)
        def _(t):
            scaled = dk[t] * SCALE
            dk[t] = scaled
            kext[t] = scaled.astype(jnp.bfloat16)
            vext[t] = dv[t].astype(jnp.bfloat16)

        copies = []
        for n, (src, wide, own_dst, part) in enumerate(
            ((kext, dk, dk_own, 0), (vext, dv, dv_own, 1))
        ):
            rim = pl.ds(part * width, width)
            copies.append(pltpu.make_async_copy(
                src.at[pl.ds(0, SPT)], low_out.at[:, :, rim], sems.at[3 * n]))
            copies.append(pltpu.make_async_copy(wide.at[own], own_dst, sems.at[3 * n + 1]))
            copies.append(pltpu.make_async_copy(
                src.at[pl.ds(SPT + own_tiles, SPT)], high_out.at[:, :, rim], sems.at[3 * n + 2]))
        for copy in copies:
            copy.start()
        for copy in copies:
            copy.wait()


def attention(heads, first_col, idx, cnt, queries, grads, keys, values, low, high):
    rows, _ = queries.shape
    own_tiles = rows // TILE
    ext_tiles = own_tiles + 2 * SPT
    width = heads * HD
    col_block = first_col // width
    assert col_block * width == first_col
    smem = pl.BlockSpec(memory_space=pltpu.SMEM)
    hbm = pl.BlockSpec(memory_space=pl.ANY)
    rim = jax.ShapeDtypeStruct((SPT, TILE, 2 * width), jnp.bfloat16)
    own = jax.ShapeDtypeStruct((own_tiles, TILE, width), jnp.float32)
    token_rows = jax.ShapeDtypeStruct((rows, width), jnp.bfloat16)
    row_block = pl.BlockSpec((TILE, width), lambda a: (a, 0))
    pairs = own_tiles * 6 * heads
    return pl.pallas_call(
        functools.partial(attention_kernel, heads, own_tiles, first_col),
        grid=(own_tiles,),
        in_specs=[
            smem, smem,
            pl.BlockSpec((TILE, width), lambda a: (a, col_block)),
            row_block, hbm, hbm, hbm, hbm,
        ],
        out_specs=[row_block, row_block, hbm, hbm, hbm, hbm],
        out_shape=[token_rows, token_rows, own, own, rim, rim],
        scratch_shapes=[
            pltpu.VMEM((ext_tiles, TILE, width), jnp.bfloat16),
            pltpu.VMEM((ext_tiles, TILE, width), jnp.bfloat16),
            pltpu.VMEM((heads, ext_tiles, HD, TILE), jnp.bfloat16),
            pltpu.VMEM((heads, ext_tiles, HD, TILE), jnp.bfloat16),
            pltpu.VMEM((heads, KSLOT, TILE, TILE), jnp.float32),
            pltpu.VMEM((ext_tiles, TILE, width), jnp.float32),
            pltpu.VMEM((ext_tiles, TILE, width), jnp.float32),
            pltpu.VMEM((heads, HD, TILE), jnp.float32),
            pltpu.VMEM((heads, HD, TILE), jnp.float32),
            pltpu.SemaphoreType.DMA((6,)),
        ],
        compiler_params=pltpu.CompilerParams(vmem_limit_bytes=56 * 1024 * 1024),
        cost_estimate=pl.CostEstimate(
            flops=pairs * 30 * TILE * TILE * HD,
            bytes_accessed=30 * rows * width,
            transcendentals=pairs * TILE * TILE,
        ),
    )(idx, cnt, queries, grads, keys, values, low, high)


def neighbours(axis):
    count = lax.axis_size(axis)
    up = [(i, i + 1) for i in range(count - 1)]
    return up, [(b, a) for a, b in up]


def scatter_heads(block):
    return lax.all_to_all(block, "head", split_axis=1, concat_axis=0, tiled=True)


def gather_heads(block):
    return lax.all_to_all(block, "head", split_axis=0, concat_axis=1, tiled=True)


def head_groups(heads_here):
    size = 2
    groups, start = [], 0
    while start < heads_here:
        groups.append((start, min(size, heads_here - start)))
        start += size
    return groups


def shards(queries, key_states, value_states, out_grads, pattern):
    row_count, col_count = queries.shape
    heads_here = col_count // HD
    rim_rows = SPT * TILE
    own_tiles = row_count // TILE
    head_devices = lax.axis_size("head")
    own_rows = out_grads.shape[0]
    first_tile = lax.axis_index("ctx") * own_tiles
    listed = lax.dynamic_slice_in_dim(pattern, first_tile, own_tiles, 0)
    allowed = listed >= 0
    idx = jnp.where(allowed, listed - (first_tile - SPT), 0).reshape(-1).astype(jnp.int32)
    cnt = jnp.sum(allowed.astype(jnp.int32), axis=1)
    up, down = neighbours("ctx")
    groups = head_groups(heads_here)
    keys_tiled = key_states.reshape(own_tiles, TILE, col_count)
    values_tiled = value_states.reshape(own_tiles, TILE, col_count)
    by_head = out_grads.reshape(own_rows, head_devices, col_count)

    lows, highs, grads = [], [], []
    for start, heads in groups:
        cols = slice(start * HD, (start + heads) * HD)
        packed = jnp.concatenate((keys_tiled[:, :, cols], values_tiled[:, :, cols]), axis=2)
        if lows:
            packed, lows[-1], highs[-1] = lax.optimization_barrier((packed, lows[-1], highs[-1]))
        lows.append(lax.ppermute(packed[own_tiles - SPT:], "ctx", up))
        highs.append(lax.ppermute(packed[:SPT], "ctx", down))
        grads.append(scatter_heads(by_head[:, :, cols].reshape(own_rows, -1)))

    attended, query_grads, key_grads, value_grads = [], [], [], []
    for group, (start, heads) in enumerate(groups):
        width = heads * HD
        out, dq, dk, dv, low, high = attention(
            heads, start * HD, idx, cnt, queries, grads[group], keys_tiled, values_tiled,
            lows[group], highs[group],
        )
        attended.append(gather_heads(out).reshape(own_rows, head_devices, width))
        query_grads.append(dq)
        from_above = lax.ppermute(low, "ctx", down)
        from_below = lax.ppermute(high, "ctx", up)
        for own, part, sums in ((dk, 0, key_grads), (dv, 1, value_grads)):
            cols = slice(part * width, (part + 1) * width)
            above = from_above[:, :, cols].astype(jnp.float32)
            below = from_below[:, :, cols].astype(jnp.float32)
            if own_tiles > SPT:
                extra = ((0, own_tiles - SPT), (0, 0), (0, 0))
                below = jnp.pad(below, extra)
                above = jnp.pad(above, (extra[0][::-1], (0, 0), (0, 0)))
            total = own + above + below
            sums.append(total.astype(jnp.bfloat16).reshape(row_count, width))
    return (
        jnp.concatenate(attended, axis=2).reshape(own_rows, head_devices * col_count),
        jnp.concatenate(query_grads, axis=1),
        jnp.concatenate(key_grads, axis=1),
        jnp.concatenate(value_grads, axis=1),
    )


def solution(mesh):
    return jax.shard_map(
        shards,
        mesh=mesh,
        in_specs=(
            P("ctx", "head"),
            P("ctx", "head"),
            P("ctx", "head"),
            P(("ctx", "head"), None),
            P(),
        ),
        out_specs=(P(("ctx", "head"), None), P("ctx", "head"), P("ctx", "head"), P("ctx", "head")),
        check_vma=False,
    )
```

```python
import functools
import math

import jax
import jax.numpy as jnp
from jax import lax
from jax.experimental import pallas as pl
from jax.experimental.pallas import tpu as pltpu
from jax.sharding import PartitionSpec as P

HD = 128
TILE = 384
SPT = 4
KSLOT = 8
SCALE = 1.0 / math.sqrt(HD)
EXP2_SCALE = SCALE * math.log2(math.e)


def dot_nn(a, b):
    return lax.dot_general(a, b, (((1,), (0,)), ((), ())), preferred_element_type=jnp.float32)


def dot_nt(a, b):
    return lax.dot_general(a, b, (((1,), (1,)), ((), ())), preferred_element_type=jnp.float32)


def fold_rows(block, op):
    return op(block.reshape(TILE // 8, 8, TILE), axis=0)


def load_extended(heads, own_tiles, first_col, rim_first, rim_width, k_hbm, v_hbm, low_hbm,
                  high_hbm, kext, vext, sems):
    width = heads * HD
    copies = []
    for n, (dst, own_src) in enumerate(((kext, k_hbm), (vext, v_hbm))):
        rim = pl.ds(n * rim_width + rim_first, width)
        own = pl.ds(first_col, width)
        copies.append(pltpu.make_async_copy(
            low_hbm.at[:, :, rim], dst.at[pl.ds(0, SPT)], sems.at[3 * n]))
        copies.append(pltpu.make_async_copy(
            own_src.at[:, :, own], dst.at[pl.ds(SPT, own_tiles)], sems.at[3 * n + 1]))
        copies.append(pltpu.make_async_copy(
            high_hbm.at[:, :, rim], dst.at[pl.ds(SPT + own_tiles, SPT)], sems.at[3 * n + 2]))
    return copies


def attention_kernel(heads, own_tiles, first_col, rim_in, rim_out, aliased, *refs):
    idx_ref, cnt_ref, q_ref, do_ref, k_hbm, v_hbm, low_hbm, high_hbm = refs[:8]
    refs = refs[8 + aliased:]
    o_ref, dq_ref, dk_own, dv_own, low_out, high_out = refs[:6]
    kext, vext, dk, dv, sems = refs[6:11]
    per_head = [refs[11 + 6 * h:17 + 6 * h] for h in range(heads)]
    kt, vt, scores, tops_at, o_acc, dq_acc = zip(*per_head)
    a = pl.program_id(0)
    ext_tiles = own_tiles + 2 * SPT
    width = heads * HD
    cols = [slice(h * HD, (h + 1) * HD) for h in range(heads)]

    @pl.when(a == 0)
    def _():
        copies = load_extended(heads, own_tiles, first_col, *rim_in, k_hbm, v_hbm, low_hbm,
                               high_hbm, kext, vext, sems)
        for copy in copies:
            copy.start()
        dk[...] = jnp.zeros_like(dk)
        dv[...] = jnp.zeros_like(dv)
        for copy in copies:
            copy.wait()

        @pl.loop(0, ext_tiles)
        def _(t):
            for h in range(heads):
                kt[h][t] = kext[t, :, cols[h]].T
                vt[h][t] = vext[t, :, cols[h]].T

    count = cnt_ref[a]

    def score_slot(s, carry):
        t = idx_ref[a * KSLOT + s]
        new = []
        blocks = [dot_nt(kext[t, :, cols[h]], q_ref[:, cols[h]]) for h in range(heads)]
        for h in range(heads):
            old, total = carry[h]
            top = jnp.maximum(old, jnp.max(fold_rows(blocks[h], jnp.max), axis=0, keepdims=True))
            weights = jnp.exp2((blocks[h] - top) * EXP2_SCALE)
            scores[h][s] = weights
            tops_at[h][s] = top
            total = total * jnp.exp2((old - top) * EXP2_SCALE) + fold_rows(weights, jnp.sum)
            new.append((top, total))
        return tuple(new)

    start = (jnp.full((1, TILE), -jnp.inf, jnp.float32), jnp.zeros((8, TILE), jnp.float32))
    stats = lax.fori_loop(0, count, score_slot, (start,) * heads)
    tops = [top for top, _ in stats]
    inverse = [1.0 / jnp.sum(total, axis=0, keepdims=True) for _, total in stats]
    for h in range(heads):
        o_acc[h][...] = jnp.zeros_like(o_acc[h])
        dq_acc[h][...] = jnp.zeros_like(dq_acc[h])

    def weights_of(h, s):
        factor = jnp.exp2((tops_at[h][s] - tops[h]) * EXP2_SCALE) * inverse[h]
        return scores[h][s] * factor

    @pl.loop(0, count)
    def _(s):
        t = idx_ref[a * KSLOT + s]
        lows = [weights_of(h, s).astype(jnp.bfloat16) for h in range(heads)]
        outs = [dot_nn(vt[h][t], lows[h]) for h in range(heads)]
        terms = [dot_nn(lows[h], do_ref[:, cols[h]]) for h in range(heads)]
        for h in range(heads):
            o_acc[h][...] += outs[h]
        dv[t] += jnp.concatenate(terms, axis=1)

    deltas = []
    for h in range(heads):
        out_t = o_acc[h][...].astype(jnp.bfloat16).astype(jnp.float32)
        grads_t = do_ref[:, cols[h]].astype(jnp.float32).T
        deltas.append(jnp.sum(out_t * grads_t, axis=0, keepdims=True))
        o_ref[:, cols[h]] = out_t.T.astype(jnp.bfloat16)

    @pl.loop(0, count)
    def _(s):
        t = idx_ref[a * KSLOT + s]
        grads = [dot_nt(vext[t, :, cols[h]], do_ref[:, cols[h]]) for h in range(heads)]
        lows = [
            (weights_of(h, s) * (grads[h] - deltas[h])).astype(jnp.bfloat16) for h in range(heads)
        ]
        terms = [dot_nn(lows[h], q_ref[:, cols[h]]) for h in range(heads)]
        query_terms = [dot_nn(kt[h][t], lows[h]) for h in range(heads)]
        dk[t] += jnp.concatenate(terms, axis=1)
        for h in range(heads):
            dq_acc[h][...] += query_terms[h]

    for h in range(heads):
        dq_ref[:, cols[h]] = (dq_acc[h][...] * SCALE).T.astype(jnp.bfloat16)

    @pl.when(a == own_tiles - 1)
    def _():
        own = pl.ds(SPT, own_tiles)
        rim_first, rim_width = rim_out

        @pl.loop(0, ext_tiles)
        def _(t):
            scaled = dk[t] * SCALE
            dk[t] = scaled
            kext[t] = scaled.astype(jnp.bfloat16)
            vext[t] = dv[t].astype(jnp.bfloat16)

        copies = []
        for n, (src, wide, own_dst) in enumerate(((kext, dk, dk_own), (vext, dv, dv_own))):
            rim = pl.ds(n * rim_width + rim_first, width)
            copies.append(pltpu.make_async_copy(
                src.at[pl.ds(0, SPT)], low_out.at[:, :, rim], sems.at[3 * n]))
            copies.append(pltpu.make_async_copy(
                wide.at[own], own_dst.at[:, :, pl.ds(rim_first, width)], sems.at[3 * n + 1]))
            copies.append(pltpu.make_async_copy(
                src.at[pl.ds(SPT + own_tiles, SPT)], high_out.at[:, :, rim], sems.at[3 * n + 2]))
        for copy in copies:
            copy.start()
        for copy in copies:
            copy.wait()


def attention(heads, first, in_span, out_span, idx, cnt, queries, grads, keys, values, low, high,
              dq_before, out_before):
    rows, all_cols = queries.shape
    own_tiles = rows // TILE
    ext_tiles = own_tiles + 2 * SPT
    width = heads * HD
    col_block = first // heads
    in_block = (first - in_span[0]) // heads
    out_block = (first - out_span[0]) // heads
    in_width, out_width = in_span[1] * HD, out_span[1] * HD
    smem = pl.BlockSpec(memory_space=pltpu.SMEM)
    hbm = pl.BlockSpec(memory_space=pl.ANY)
    rim = jax.ShapeDtypeStruct((SPT, TILE, 2 * out_width), jnp.bfloat16)
    own = jax.ShapeDtypeStruct((own_tiles, TILE, out_width), jnp.float32)
    out_shape = [
        jax.ShapeDtypeStruct((rows, out_width), jnp.bfloat16),
        jax.ShapeDtypeStruct((rows, all_cols), jnp.bfloat16),
        own, own, rim, rim,
    ]
    before, aliases = [], {}
    if dq_before is not None:
        aliases[8 + len(before)] = 1
        before.append(dq_before)
    if out_before is not None:
        for at, array in zip((0, 2, 3, 4, 5), out_before):
            aliases[8 + len(before)] = at
            before.append(array)
    pairs = own_tiles * 6 * heads
    per_head = [
        pltpu.VMEM((ext_tiles, HD, TILE), jnp.bfloat16),
        pltpu.VMEM((ext_tiles, HD, TILE), jnp.bfloat16),
        pltpu.VMEM((KSLOT, TILE, TILE), jnp.float32),
        pltpu.VMEM((KSLOT, 1, TILE), jnp.float32),
        pltpu.VMEM((HD, TILE), jnp.float32),
        pltpu.VMEM((HD, TILE), jnp.float32),
    ]
    out, dq, *rest = pl.pallas_call(
        functools.partial(
            attention_kernel, heads, own_tiles, first * HD,
            ((first - in_span[0]) * HD, in_width), ((first - out_span[0]) * HD, out_width),
            len(before),
        ),
        grid=(own_tiles,),
        in_specs=[
            smem, smem,
            pl.BlockSpec((TILE, width), lambda a: (a, col_block)),
            pl.BlockSpec((TILE, width), lambda a: (a, in_block)),
            hbm, hbm, hbm, hbm,
        ] + [hbm] * len(before),
        out_specs=[
            pl.BlockSpec((TILE, width), lambda a: (a, out_block)),
            pl.BlockSpec((TILE, width), lambda a: (a, col_block)),
            hbm, hbm, hbm, hbm,
        ],
        out_shape=out_shape,
        input_output_aliases=aliases,
        scratch_shapes=[
            pltpu.VMEM((ext_tiles, TILE, width), jnp.bfloat16),
            pltpu.VMEM((ext_tiles, TILE, width), jnp.bfloat16),
            pltpu.VMEM((ext_tiles, TILE, width), jnp.float32),
            pltpu.VMEM((ext_tiles, TILE, width), jnp.float32),
            pltpu.SemaphoreType.DMA((6,)),
        ] + per_head * heads,
        compiler_params=pltpu.CompilerParams(vmem_limit_bytes=56 * 1024 * 1024),
        cost_estimate=pl.CostEstimate(
            flops=pairs * 30 * TILE * TILE * HD,
            bytes_accessed=30 * rows * width,
            transcendentals=pairs * TILE * TILE,
        ),
    )(idx, cnt, queries, grads, keys, values, low, high, *before)
    return dq, (out, *rest)


def finish_kernel(own_tiles, k_own, v_own, ka, va, kb, vb, *refs):
    dk_ref, dv_ref = refs[-2:]
    a = pl.program_id(0)
    above = jnp.where(a >= own_tiles - SPT, 1.0, 0.0)
    below = jnp.where(a < SPT, 1.0, 0.0)
    for own, hi, lo, out in ((k_own, ka, kb, dk_ref), (v_own, va, vb, dv_ref)):
        total = own[0] + above * hi[0].astype(jnp.float32) + below * lo[0].astype(jnp.float32)
        out[...] = total.astype(jnp.bfloat16)


def finish(span, all_cols, dk_own, dv_own, from_above, from_below, before):
    own_tiles = dk_own.shape[0]
    width = span[1] * HD
    col_block = span[0] // span[1]
    own = pl.BlockSpec((1, TILE, width), lambda a: (a, 0, 0))

    def rim(shift, part):
        return pl.BlockSpec(
            (1, TILE, width), lambda a: (jnp.clip(a - shift, 0, SPT - 1), 0, part))

    out = pl.BlockSpec((TILE, width), lambda a: (a, col_block))
    shape = jax.ShapeDtypeStruct((own_tiles * TILE, all_cols), jnp.bfloat16)
    gap = own_tiles - SPT
    return pl.pallas_call(
        functools.partial(finish_kernel, own_tiles),
        grid=(own_tiles,),
        in_specs=[own, own, rim(gap, 0), rim(gap, 1), rim(0, 0), rim(0, 1)]
        + [pl.BlockSpec(memory_space=pl.ANY)] * len(before),
        out_specs=[out, out],
        out_shape=[shape, shape],
        input_output_aliases={6 + n: n for n in range(len(before))},
        compiler_params=pltpu.CompilerParams(vmem_limit_bytes=32 * 1024 * 1024),
        cost_estimate=pl.CostEstimate(
            flops=4 * own_tiles * TILE * width,
            bytes_accessed=20 * own_tiles * TILE * width,
            transcendentals=0,
        ),
    )(dk_own, dv_own, from_above, from_above, from_below, from_below, *before)


def neighbours(axis):
    count = lax.axis_size(axis)
    up = [(i, i + 1) for i in range(count - 1)]
    return up, [(b, a) for a, b in up]


def scatter_heads(block):
    return lax.all_to_all(block, "head", split_axis=1, concat_axis=0, tiled=True)


def gather_heads(block):
    return lax.all_to_all(block, "head", split_axis=0, concat_axis=1, tiled=True)


def head_plan(heads_here):
    size = 2
    groups = [(at, min(size, heads_here - at)) for at in range(0, heads_here, size)]
    first, last = groups[0], groups[-1]
    in_spans, out_spans = [first], [(0, last[0]), last]
    if heads_here > first[1]:
        in_spans.append((first[1], heads_here - first[1]))
    else:
        out_spans = [last]
    return groups, in_spans, out_spans


def span_of(head, spans):
    return [n for n, (at, count) in enumerate(spans) if at <= head < at + count][0]


def shards(queries, key_states, value_states, out_grads, pattern):
    row_count, col_count = queries.shape
    own_tiles = row_count // TILE
    head_devices = lax.axis_size("head")
    own_rows = out_grads.shape[0]
    first_tile = lax.axis_index("ctx") * own_tiles
    listed = lax.dynamic_slice_in_dim(pattern, first_tile, own_tiles, 0)
    allowed = listed >= 0
    idx = jnp.where(allowed, listed - (first_tile - SPT), 0).reshape(-1).astype(jnp.int32)
    cnt = jnp.sum(allowed.astype(jnp.int32), axis=1)
    up, down = neighbours("ctx")
    groups, in_spans, out_spans = head_plan(col_count // HD)
    keys_tiled = key_states.reshape(own_tiles, TILE, col_count)
    values_tiled = value_states.reshape(own_tiles, TILE, col_count)
    by_head = out_grads.reshape(own_rows, head_devices, col_count)

    lows, highs, grads = [], [], []
    for at, heads in in_spans:
        cols = slice(at * HD, (at + heads) * HD)
        packed = jnp.concatenate((keys_tiled[:, :, cols], values_tiled[:, :, cols]), axis=2)
        grad_part = by_head[:, :, cols]
        if lows:
            packed, grad_part, lows[-1], highs[-1], grads[-1] = lax.optimization_barrier(
                (packed, grad_part, lows[-1], highs[-1], grads[-1]))
        lows.append(lax.ppermute(packed[own_tiles - SPT:], "ctx", up))
        highs.append(lax.ppermute(packed[:SPT], "ctx", down))
        grads.append(scatter_heads(grad_part.reshape(own_rows, -1)))

    dq, parts = None, [None] * len(out_spans)
    for at, heads in groups:
        source, target = span_of(at, in_spans), span_of(at, out_spans)
        dq, parts[target] = attention(
            heads, at, in_spans[source], out_spans[target], idx, cnt, queries, grads[source],
            keys_tiled, values_tiled, lows[source], highs[source], dq, parts[target],
        )

    attended, sums = [], ()
    for span, (out, dk_own, dv_own, low, high) in zip(out_spans, parts):
        attended.append(gather_heads(out).reshape(own_rows, head_devices, span[1] * HD))
        from_above = lax.ppermute(low, "ctx", down)
        from_below = lax.ppermute(high, "ctx", up)
        sums = finish(span, col_count, dk_own, dv_own, from_above, from_below, sums)
    attended = jnp.concatenate(attended, axis=2).reshape(own_rows, head_devices * col_count)
    return attended, dq, sums[0], sums[1]


def solution(mesh):
    return jax.shard_map(
        shards,
        mesh=mesh,
        in_specs=(
            P("ctx", "head"),
            P("ctx", "head"),
            P("ctx", "head"),
            P(("ctx", "head"), None),
            P(),
        ),
        out_specs=(P(("ctx", "head"), None), P("ctx", "head"), P("ctx", "head"), P("ctx", "head")),
        check_vma=False,
    )
```

```python
import functools
import math

import jax
import jax.numpy as jnp
from jax import lax
from jax.experimental import pallas as pl
from jax.experimental.pallas import tpu as pltpu
from jax.sharding import PartitionSpec as P

HD = 128
TILE = 384
SPT = 4
KSLOT = 8
SCALE = 1.0 / math.sqrt(HD)
EXP2_SCALE = SCALE * math.log2(math.e)


def dot_nn(a, b):
    return lax.dot_general(a, b, (((1,), (0,)), ((), ())), preferred_element_type=jnp.float32)


def dot_nt(a, b):
    return lax.dot_general(a, b, (((1,), (1,)), ((), ())), preferred_element_type=jnp.float32)


def fold_rows(block, op):
    return op(block.reshape(TILE // 8, 8, TILE), axis=0)


def load_extended(heads, own_tiles, first_col, rim_first, rim_width, k_hbm, v_hbm, low_hbm,
                  high_hbm, kext, vext, sems):
    width = heads * HD
    copies = []
    for n, (dst, own_src) in enumerate(((kext, k_hbm), (vext, v_hbm))):
        rim = pl.ds(n * rim_width + rim_first, width)
        own = pl.ds(first_col, width)
        copies.append(pltpu.make_async_copy(
            low_hbm.at[:, :, rim], dst.at[pl.ds(0, SPT)], sems.at[3 * n]))
        copies.append(pltpu.make_async_copy(
            own_src.at[:, :, own], dst.at[pl.ds(SPT, own_tiles)], sems.at[3 * n + 1]))
        copies.append(pltpu.make_async_copy(
            high_hbm.at[:, :, rim], dst.at[pl.ds(SPT + own_tiles, SPT)], sems.at[3 * n + 2]))
    return copies


def attention_kernel(heads, own_tiles, first_col, rim_in, rim_out, aliased, *refs):
    idx_ref, cnt_ref, q_ref, do_ref, k_hbm, v_hbm, low_hbm, high_hbm = refs[:8]
    refs = refs[8 + aliased:]
    o_ref, dq_ref, dk_own, dv_own, low_out, high_out = refs[:6]
    kext, vext, sems = refs[6:9]
    per_head = [refs[9 + 8 * h:17 + 8 * h] for h in range(heads)]
    kt, vt, scores, lows, dk, dv, o_acc, dq_acc = zip(*per_head)
    a = pl.program_id(0)
    ext_tiles = own_tiles + 2 * SPT
    width = heads * HD
    cols = [slice(h * HD, (h + 1) * HD) for h in range(heads)]

    @pl.when(a == 0)
    def _():
        copies = load_extended(heads, own_tiles, first_col, *rim_in, k_hbm, v_hbm, low_hbm,
                               high_hbm, kext, vext, sems)
        for copy in copies:
            copy.start()
        for total in dk + dv:
            total[...] = jnp.zeros_like(total)
        for copy in copies:
            copy.wait()

        @pl.loop(0, ext_tiles)
        def _(t):
            for h in range(heads):
                kt[h][t] = kext[t, :, cols[h]].T
                vt[h][t] = vext[t, :, cols[h]].T

    count = cnt_ref[a]

    tops, inverse, deltas = [None] * heads, [None] * heads, [None] * heads

    def score_stage(h, s, t, top):
        block = dot_nt(kext[t, :, cols[h]], q_ref[:, cols[h]])
        scores[h][s] = block
        return jnp.maximum(top, fold_rows(block, jnp.max))

    def exp_stage(h, s, t, total):
        block = jnp.exp2((scores[h][s] - tops[h]) * EXP2_SCALE)
        scores[h][s] = block
        return total + fold_rows(block, jnp.sum)

    def value_stage(h, s, t, carry):
        low = (scores[h][s] * inverse[h]).astype(jnp.bfloat16)
        o_acc[h][...] += dot_nn(vt[h][t], low)
        dv[h][t] += dot_nn(low, do_ref[:, cols[h]])
        return carry

    def grad_stage(h, s, t, carry):
        grads = dot_nt(vext[t, :, cols[h]], do_ref[:, cols[h]])
        lows[h][s] = ((scores[h][s] * inverse[h]) * (grads - deltas[h])).astype(jnp.bfloat16)
        return carry

    def key_stage(h, s, t, carry):
        low = lows[h][s]
        dk[h][t] += dot_nn(low, q_ref[:, cols[h]])
        dq_acc[h][...] += dot_nn(kt[h][t], low)
        return carry

    stages = (score_stage, exp_stage, value_stage, grad_stage, key_stage)

    def begin(h, stage):
        if stage == 0:
            return jnp.full((8, TILE), -jnp.inf, jnp.float32)
        if stage == 1:
            return jnp.zeros((8, TILE), jnp.float32)
        if stage == 2:
            o_acc[h][...] = jnp.zeros_like(o_acc[h])
        if stage == 4:
            dq_acc[h][...] = jnp.zeros_like(dq_acc[h])
        return jnp.int32(0)

    def finish_stage(h, stage, carry):
        if stage == 0:
            tops[h] = jnp.max(carry, axis=0, keepdims=True)
        if stage == 1:
            inverse[h] = 1.0 / jnp.sum(carry, axis=0, keepdims=True)
        if stage == 2:
            out_t = o_acc[h][...].astype(jnp.bfloat16).astype(jnp.float32)
            grads_t = do_ref[:, cols[h]].astype(jnp.float32).T
            deltas[h] = jnp.sum(out_t * grads_t, axis=0, keepdims=True)
            o_ref[:, cols[h]] = out_t.T.astype(jnp.bfloat16)
        if stage == 4:
            dq_ref[:, cols[h]] = (dq_acc[h][...] * SCALE).T.astype(jnp.bfloat16)

    for step in range(len(stages) + heads - 1):
        active = [(h, step - h) for h in range(heads) if 0 <= step - h < len(stages)]

        def slot(s, carry, active=active):
            t = idx_ref[a * KSLOT + s]
            return tuple(
                stages[stage](h, s, t, part) for (h, stage), part in zip(active, carry)
            )

        done = lax.fori_loop(0, count, slot, tuple(begin(h, stage) for h, stage in active))
        for (h, stage), part in zip(active, done):
            finish_stage(h, stage, part)

    @pl.when(a == own_tiles - 1)
    def _():
        own = pl.ds(SPT, own_tiles)
        rim_first, rim_width = rim_out

        @pl.loop(0, ext_tiles)
        def _(t):
            for h in range(heads):
                scaled = dk[h][t] * SCALE
                dk[h][t] = scaled
                kext[t, :, cols[h]] = scaled.astype(jnp.bfloat16)
                vext[t, :, cols[h]] = dv[h][t].astype(jnp.bfloat16)

        copies = []
        for n, (src, wide, own_dst) in enumerate(((kext, dk, dk_own), (vext, dv, dv_own))):
            rim = pl.ds(n * rim_width + rim_first, width)
            first = n * (2 + heads)
            copies.append(pltpu.make_async_copy(
                src.at[pl.ds(0, SPT)], low_out.at[:, :, rim], sems.at[first]))
            copies.append(pltpu.make_async_copy(
                src.at[pl.ds(SPT + own_tiles, SPT)], high_out.at[:, :, rim], sems.at[first + 1]))
            for h in range(heads):
                copies.append(pltpu.make_async_copy(
                    wide[h].at[own], own_dst.at[:, :, pl.ds(rim_first + h * HD, HD)],
                    sems.at[first + 2 + h]))
        for copy in copies:
            copy.start()
        for copy in copies:
            copy.wait()


def attention(heads, first, in_span, out_span, idx, cnt, queries, grads, keys, values, low, high,
              dq_before, out_before):
    rows, all_cols = queries.shape
    own_tiles = rows // TILE
    ext_tiles = own_tiles + 2 * SPT
    width = heads * HD
    col_block = first // heads
    in_block = (first - in_span[0]) // heads
    out_block = (first - out_span[0]) // heads
    in_width, out_width = in_span[1] * HD, out_span[1] * HD
    smem = pl.BlockSpec(memory_space=pltpu.SMEM)
    hbm = pl.BlockSpec(memory_space=pl.ANY)
    rim = jax.ShapeDtypeStruct((SPT, TILE, 2 * out_width), jnp.bfloat16)
    own = jax.ShapeDtypeStruct((own_tiles, TILE, out_width), jnp.float32)
    out_shape = [
        jax.ShapeDtypeStruct((rows, out_width), jnp.bfloat16),
        jax.ShapeDtypeStruct((rows, all_cols), jnp.bfloat16),
        own, own, rim, rim,
    ]
    before, aliases = [], {}
    if dq_before is not None:
        aliases[8 + len(before)] = 1
        before.append(dq_before)
    if out_before is not None:
        for at, array in zip((0, 2, 3, 4, 5), out_before):
            aliases[8 + len(before)] = at
            before.append(array)
    pairs = own_tiles * 6 * heads
    per_head = [
        pltpu.VMEM((ext_tiles, HD, TILE), jnp.bfloat16),
        pltpu.VMEM((ext_tiles, HD, TILE), jnp.bfloat16),
        pltpu.VMEM((KSLOT, TILE, TILE), jnp.float32),
        pltpu.VMEM((KSLOT, TILE, TILE), jnp.bfloat16),
        pltpu.VMEM((ext_tiles, TILE, HD), jnp.float32),
        pltpu.VMEM((ext_tiles, TILE, HD), jnp.float32),
        pltpu.VMEM((HD, TILE), jnp.float32),
        pltpu.VMEM((HD, TILE), jnp.float32),
    ]
    out, dq, *rest = pl.pallas_call(
        functools.partial(
            attention_kernel, heads, own_tiles, first * HD,
            ((first - in_span[0]) * HD, in_width), ((first - out_span[0]) * HD, out_width),
            len(before),
        ),
        grid=(own_tiles,),
        in_specs=[
            smem, smem,
            pl.BlockSpec((TILE, width), lambda a: (a, col_block)),
            pl.BlockSpec((TILE, width), lambda a: (a, in_block)),
            hbm, hbm, hbm, hbm,
        ] + [hbm] * len(before),
        out_specs=[
            pl.BlockSpec((TILE, width), lambda a: (a, out_block)),
            pl.BlockSpec((TILE, width), lambda a: (a, col_block)),
            hbm, hbm, hbm, hbm,
        ],
        out_shape=out_shape,
        input_output_aliases=aliases,
        scratch_shapes=[
            pltpu.VMEM((ext_tiles, TILE, width), jnp.bfloat16),
            pltpu.VMEM((ext_tiles, TILE, width), jnp.bfloat16),
            pltpu.SemaphoreType.DMA((6 + 2 * heads,)),
        ] + per_head * heads,
        compiler_params=pltpu.CompilerParams(vmem_limit_bytes=56 * 1024 * 1024),
        cost_estimate=pl.CostEstimate(
            flops=pairs * 30 * TILE * TILE * HD,
            bytes_accessed=30 * rows * width,
            transcendentals=pairs * TILE * TILE,
        ),
    )(idx, cnt, queries, grads, keys, values, low, high, *before)
    return dq, (out, *rest)


def finish_kernel(own_tiles, k_own, v_own, ka, va, kb, vb, *refs):
    dk_ref, dv_ref = refs[-2:]
    a = pl.program_id(0)
    above = jnp.where(a >= own_tiles - SPT, 1.0, 0.0)
    below = jnp.where(a < SPT, 1.0, 0.0)
    for own, hi, lo, out in ((k_own, ka, kb, dk_ref), (v_own, va, vb, dv_ref)):
        total = own[0] + above * hi[0].astype(jnp.float32) + below * lo[0].astype(jnp.float32)
        out[...] = total.astype(jnp.bfloat16)


def finish(span, all_cols, dk_own, dv_own, from_above, from_below, before):
    own_tiles = dk_own.shape[0]
    width = span[1] * HD
    col_block = span[0] // span[1]
    own = pl.BlockSpec((1, TILE, width), lambda a: (a, 0, 0))

    def rim(shift, part):
        return pl.BlockSpec(
            (1, TILE, width), lambda a: (jnp.clip(a - shift, 0, SPT - 1), 0, part))

    out = pl.BlockSpec((TILE, width), lambda a: (a, col_block))
    shape = jax.ShapeDtypeStruct((own_tiles * TILE, all_cols), jnp.bfloat16)
    gap = own_tiles - SPT
    return pl.pallas_call(
        functools.partial(finish_kernel, own_tiles),
        grid=(own_tiles,),
        in_specs=[own, own, rim(gap, 0), rim(gap, 1), rim(0, 0), rim(0, 1)]
        + [pl.BlockSpec(memory_space=pl.ANY)] * len(before),
        out_specs=[out, out],
        out_shape=[shape, shape],
        input_output_aliases={6 + n: n for n in range(len(before))},
        compiler_params=pltpu.CompilerParams(vmem_limit_bytes=32 * 1024 * 1024),
        cost_estimate=pl.CostEstimate(
            flops=4 * own_tiles * TILE * width,
            bytes_accessed=20 * own_tiles * TILE * width,
            transcendentals=0,
        ),
    )(dk_own, dv_own, from_above, from_above, from_below, from_below, *before)


def neighbours(axis):
    count = lax.axis_size(axis)
    up = [(i, i + 1) for i in range(count - 1)]
    return up, [(b, a) for a, b in up]


def swap_blocks(blocks):
    return lax.all_to_all(blocks, "head", split_axis=0, concat_axis=0, tiled=True)


def swap_blocks_by_permutes(blocks):
    count = lax.axis_size("head")
    me = lax.axis_index("head")
    pieces = [lax.dynamic_index_in_dim(blocks, me, 0, keepdims=False)]
    for turn in range(1, count):
        piece = lax.dynamic_index_in_dim(blocks, lax.rem(me + turn, count), 0, keepdims=False)
        route = [(i, (i + turn) % count) for i in range(count)]
        pieces.append(lax.ppermute(piece, "head", route))
    ring = jnp.stack(pieces[::-1] * 2)
    return lax.dynamic_slice_in_dim(ring, count - 1 - me, count, 0)


def head_plan(heads_here):
    size = 2
    groups = [(at, min(size, heads_here - at)) for at in range(0, heads_here, size)]
    first, last = groups[0], groups[-1]
    in_spans, out_spans = [first], [(0, last[0]), last]
    if heads_here > first[1]:
        in_spans.append((first[1], heads_here - first[1]))
    else:
        out_spans = [last]
    return groups, in_spans, out_spans


def span_of(head, spans):
    return [n for n, (at, count) in enumerate(spans) if at <= head < at + count][0]


def shards(queries, key_states, value_states, out_grads, pattern):
    row_count, col_count = queries.shape
    own_tiles = row_count // TILE
    head_devices = lax.axis_size("head")
    own_rows = out_grads.shape[0]
    first_tile = lax.axis_index("ctx") * own_tiles
    listed = lax.dynamic_slice_in_dim(pattern, first_tile, own_tiles, 0)
    allowed = listed >= 0
    idx = jnp.where(allowed, listed - (first_tile - SPT), 0).reshape(-1).astype(jnp.int32)
    cnt = jnp.sum(allowed.astype(jnp.int32), axis=1)
    up, down = neighbours("ctx")
    groups, in_spans, out_spans = head_plan(col_count // HD)
    keys_tiled = key_states.reshape(own_tiles, TILE, col_count)
    values_tiled = value_states.reshape(own_tiles, TILE, col_count)

    lows, highs, grads = [], [], []
    for at, heads in in_spans:
        cols = slice(at * HD, (at + heads) * HD)
        packed = jnp.concatenate((keys_tiled[:, :, cols], values_tiled[:, :, cols]), axis=2)
        grad_part = jnp.stack([
            out_grads[:, n * col_count + at * HD:n * col_count + (at + heads) * HD]
            for n in range(head_devices)
        ])
        if lows:
            packed, grad_part, lows[-1], highs[-1], grads[-1] = lax.optimization_barrier(
                (packed, grad_part, lows[-1], highs[-1], grads[-1]))
        lows.append(lax.ppermute(packed[own_tiles - SPT:], "ctx", up))
        highs.append(lax.ppermute(packed[:SPT], "ctx", down))
        grads.append(swap_blocks(grad_part).reshape(row_count, heads * HD))

    dq, parts = None, [None] * len(out_spans)
    for at, heads in groups:
        source, target = span_of(at, in_spans), span_of(at, out_spans)
        dq, parts[target] = attention(
            heads, at, in_spans[source], out_spans[target], idx, cnt, queries, grads[source],
            keys_tiled, values_tiled, lows[source], highs[source], dq, parts[target],
        )

    attended, sums = [], ()
    for n, (span, (out, dk_own, dv_own, low, high)) in enumerate(zip(out_spans, parts)):
        swap = swap_blocks if n + 1 == len(out_spans) else swap_blocks_by_permutes
        attended.append(swap(out.reshape(head_devices, own_rows, span[1] * HD)))
        from_above = lax.ppermute(low, "ctx", down)
        from_below = lax.ppermute(high, "ctx", up)
        sums = finish(span, col_count, dk_own, dv_own, from_above, from_below, sums)
    attended = jnp.concatenate(
        [part[n] for n in range(head_devices) for part in attended], axis=1)
    return attended, dq, sums[0], sums[1]


def solution(mesh):
    return jax.shard_map(
        shards,
        mesh=mesh,
        in_specs=(
            P("ctx", "head"),
            P("ctx", "head"),
            P("ctx", "head"),
            P(("ctx", "head"), None),
            P(),
        ),
        out_specs=(P(("ctx", "head"), None), P("ctx", "head"), P("ctx", "head"), P("ctx", "head")),
        check_vma=False,
    )
```

```python
import functools
import math

import jax
import jax.numpy as jnp
from jax import lax
from jax.experimental import pallas as pl
from jax.experimental.pallas import tpu as pltpu
from jax.sharding import PartitionSpec as P

HD = 128
TILE = 384
SPT = 4
KSLOT = 8
SCALE = 1.0 / math.sqrt(HD)
EXP2_SCALE = SCALE * math.log2(math.e)


def dot_nn(a, b):
    return lax.dot_general(a, b, (((1,), (0,)), ((), ())), preferred_element_type=jnp.float32)


def dot_nt(a, b):
    return lax.dot_general(a, b, (((1,), (1,)), ((), ())), preferred_element_type=jnp.float32)


def fold_rows(block, op):
    return op(block.reshape(TILE // 8, 8, TILE), axis=0)


def load_extended(heads, own_tiles, first_col, rim_first, rim_width, k_hbm, v_hbm, low_hbm,
                  high_hbm, kext, vext, sems):
    width = heads * HD
    copies = []
    for n, (dst, own_src) in enumerate(((kext, k_hbm), (vext, v_hbm))):
        rim = pl.ds(n * rim_width + rim_first, width)
        own = pl.ds(first_col, width)
        copies.append(pltpu.make_async_copy(
            low_hbm.at[:, :, rim], dst.at[pl.ds(0, SPT)], sems.at[3 * n]))
        copies.append(pltpu.make_async_copy(
            own_src.at[:, :, own], dst.at[pl.ds(SPT, own_tiles)], sems.at[3 * n + 1]))
        copies.append(pltpu.make_async_copy(
            high_hbm.at[:, :, rim], dst.at[pl.ds(SPT + own_tiles, SPT)], sems.at[3 * n + 2]))
    return copies


def attention_kernel(heads, own_tiles, first_col, rim_in, rim_out, aliased, *refs):
    idx_ref, cnt_ref, q_ref, do_ref, k_hbm, v_hbm, low_hbm, high_hbm = refs[:8]
    refs = refs[8 + aliased:]
    o_ref, dq_ref, dk_own, dv_own, low_out, high_out = refs[:6]
    kext, vext, dk, dv, q_wide, do_wide, sems = refs[6:13]
    per_head = [refs[13 + 6 * h:19 + 6 * h] for h in range(heads)]
    kt, vt, scores, tops_at, o_acc, dq_acc = zip(*per_head)
    a = pl.program_id(0)
    ext_tiles = own_tiles + 2 * SPT
    width = heads * HD
    cols = [slice(h * HD, (h + 1) * HD) for h in range(heads)]

    @pl.when(a == 0)
    def _():
        copies = load_extended(heads, own_tiles, first_col, *rim_in, k_hbm, v_hbm, low_hbm,
                               high_hbm, kext, vext, sems)
        for copy in copies:
            copy.start()
        q_wide[...] = jnp.zeros_like(q_wide)
        do_wide[...] = jnp.zeros_like(do_wide)
        dk[...] = jnp.zeros_like(dk)
        dv[...] = jnp.zeros_like(dv)
        for copy in copies:
            copy.wait()

        @pl.loop(0, ext_tiles)
        def _(t):
            for h in range(heads):
                kt[h][t] = kext[t, :, cols[h]].T
                vt[h][t] = vext[t, :, cols[h]].T

    count = cnt_ref[a]
    for h in range(heads):
        for wide, ref in ((q_wide, q_ref), (do_wide, do_ref)):
            wide[h * TILE:(h + 1) * TILE, cols[h]] = ref[:, cols[h]]
    split = [slice(h * TILE, (h + 1) * TILE) for h in range(heads)]

    def over_slots(body, carry):
        def double(i, carry):
            return body((2 * i, 2 * i + 1), carry)

        def single(s, carry):
            return body((s,), carry)

        carry = lax.fori_loop(0, count // 2, double, carry)
        return lax.fori_loop(count // 2 * 2, count, single, carry)

    def tiles(slots):
        return [idx_ref[a * KSLOT + s] for s in slots]

    def score_slots(slots, carry):
        blocks = [dot_nt(kext[t], q_wide[...]) for t in tiles(slots)]
        new = []
        for h in range(heads):
            old, total = carry[h]
            parts = [block[:, split[h]] for block in blocks]
            peak = functools.reduce(jnp.maximum, [fold_rows(part, jnp.max) for part in parts])
            top = jnp.maximum(old, jnp.max(peak, axis=0, keepdims=True))
            total = total * jnp.exp2((old - top) * EXP2_SCALE)
            for s, part in zip(slots, parts):
                weights = jnp.exp2((part - top) * EXP2_SCALE)
                scores[h][s] = weights
                tops_at[h][s] = top
                total = total + fold_rows(weights, jnp.sum)
            new.append((top, total))
        return tuple(new)

    start = (jnp.full((1, TILE), -jnp.inf, jnp.float32), jnp.zeros((8, TILE), jnp.float32))
    stats = over_slots(score_slots, (start,) * heads)
    tops = [top for top, _ in stats]
    inverse = [1.0 / jnp.sum(total, axis=0, keepdims=True) for _, total in stats]
    for h in range(heads):
        o_acc[h][...] = jnp.zeros_like(o_acc[h])
        dq_acc[h][...] = jnp.zeros_like(dq_acc[h])

    def weights_of(h, s):
        factor = jnp.exp2((tops_at[h][s] - tops[h]) * EXP2_SCALE) * inverse[h]
        return scores[h][s] * factor

    def joined(blocks, axis):
        return blocks[0] if len(blocks) == 1 else jnp.concatenate(blocks, axis=axis)

    def value_slots(slots, carry):
        at = tiles(slots)
        lows = [[weights_of(h, s).astype(jnp.bfloat16) for h in range(heads)] for s in slots]
        for t, low in zip(at, lows):
            dv[t] += dot_nn(joined(low, 1), do_wide[...])
        for h in range(heads):
            o_acc[h][...] += dot_nn(
                joined([vt[h][t] for t in at], 1), joined([low[h] for low in lows], 0))
        return carry

    over_slots(value_slots, jnp.int32(0))

    deltas = []
    for h in range(heads):
        out_t = o_acc[h][...].astype(jnp.bfloat16).astype(jnp.float32)
        grads_t = do_ref[:, cols[h]].astype(jnp.float32).T
        deltas.append(jnp.sum(out_t * grads_t, axis=0, keepdims=True))
        o_ref[:, cols[h]] = out_t.T.astype(jnp.bfloat16)

    def key_slots(slots, carry):
        at = tiles(slots)
        grads = [dot_nt(vext[t], do_wide[...]) for t in at]
        lows = [
            [
                (weights_of(h, s) * (grad[:, split[h]] - deltas[h])).astype(jnp.bfloat16)
                for h in range(heads)
            ]
            for s, grad in zip(slots, grads)
        ]
        for t, low in zip(at, lows):
            dk[t] += dot_nn(joined(low, 1), q_wide[...])
        for h in range(heads):
            dq_acc[h][...] += dot_nn(
                joined([kt[h][t] for t in at], 1), joined([low[h] for low in lows], 0))
        return carry

    over_slots(key_slots, jnp.int32(0))

    for h in range(heads):
        dq_ref[:, cols[h]] = (dq_acc[h][...] * SCALE).T.astype(jnp.bfloat16)

    @pl.when(a == own_tiles - 1)
    def _():
        own = pl.ds(SPT, own_tiles)
        rim_first, rim_width = rim_out

        @pl.loop(0, ext_tiles)
        def _(t):
            scaled = dk[t] * SCALE
            dk[t] = scaled
            kext[t] = scaled.astype(jnp.bfloat16)
            vext[t] = dv[t].astype(jnp.bfloat16)

        copies = []
        for n, (src, wide, own_dst) in enumerate(((kext, dk, dk_own), (vext, dv, dv_own))):
            rim = pl.ds(n * rim_width + rim_first, width)
            copies.append(pltpu.make_async_copy(
                src.at[pl.ds(0, SPT)], low_out.at[:, :, rim], sems.at[3 * n]))
            copies.append(pltpu.make_async_copy(
                wide.at[own], own_dst.at[:, :, pl.ds(rim_first, width)], sems.at[3 * n + 1]))
            copies.append(pltpu.make_async_copy(
                src.at[pl.ds(SPT + own_tiles, SPT)], high_out.at[:, :, rim], sems.at[3 * n + 2]))
        for copy in copies:
            copy.start()
        for copy in copies:
            copy.wait()


def attention(heads, first, in_span, out_span, idx, cnt, queries, grads, keys, values, low, high,
              dq_before, out_before):
    rows, all_cols = queries.shape
    own_tiles = rows // TILE
    ext_tiles = own_tiles + 2 * SPT
    width = heads * HD
    col_block = first // heads
    in_block = (first - in_span[0]) // heads
    in_width, out_width = in_span[1] * HD, out_span[1] * HD
    smem = pl.BlockSpec(memory_space=pltpu.SMEM)
    hbm = pl.BlockSpec(memory_space=pl.ANY)
    rim = jax.ShapeDtypeStruct((SPT, TILE, 2 * out_width), jnp.bfloat16)
    own = jax.ShapeDtypeStruct((own_tiles, TILE, out_width), jnp.float32)
    out_shape = [
        jax.ShapeDtypeStruct((rows, width), jnp.bfloat16),
        jax.ShapeDtypeStruct((rows, all_cols), jnp.bfloat16),
        own, own, rim, rim,
    ]
    before, aliases = [], {}
    if dq_before is not None:
        aliases[8 + len(before)] = 1
        before.append(dq_before)
    if out_before is not None:
        for at, array in zip((2, 3, 4, 5), out_before):
            aliases[8 + len(before)] = at
            before.append(array)
    pairs = own_tiles * 6 * heads
    per_head = [
        pltpu.VMEM((ext_tiles, HD, TILE), jnp.bfloat16),
        pltpu.VMEM((ext_tiles, HD, TILE), jnp.bfloat16),
        pltpu.VMEM((KSLOT, TILE, TILE), jnp.float32),
        pltpu.VMEM((KSLOT, 1, TILE), jnp.float32),
        pltpu.VMEM((HD, TILE), jnp.float32),
        pltpu.VMEM((HD, TILE), jnp.float32),
    ]
    out, dq, *rest = pl.pallas_call(
        functools.partial(
            attention_kernel, heads, own_tiles, first * HD,
            ((first - in_span[0]) * HD, in_width), ((first - out_span[0]) * HD, out_width),
            len(before),
        ),
        grid=(own_tiles,),
        in_specs=[
            smem, smem,
            pl.BlockSpec((TILE, width), lambda a: (a, col_block)),
            pl.BlockSpec((TILE, width), lambda a: (a, in_block)),
            hbm, hbm, hbm, hbm,
        ] + [hbm] * len(before),
        out_specs=[
            pl.BlockSpec((TILE, width), lambda a: (a, 0)),
            pl.BlockSpec((TILE, width), lambda a: (a, col_block)),
            hbm, hbm, hbm, hbm,
        ],
        out_shape=out_shape,
        input_output_aliases=aliases,
        scratch_shapes=[
            pltpu.VMEM((ext_tiles, TILE, width), jnp.bfloat16),
            pltpu.VMEM((ext_tiles, TILE, width), jnp.bfloat16),
            pltpu.VMEM((ext_tiles, TILE, width), jnp.float32),
            pltpu.VMEM((ext_tiles, TILE, width), jnp.float32),
            pltpu.VMEM((heads * TILE, width), jnp.bfloat16),
            pltpu.VMEM((heads * TILE, width), jnp.bfloat16),
            pltpu.SemaphoreType.DMA((6,)),
        ] + per_head * heads,
        compiler_params=pltpu.CompilerParams(vmem_limit_bytes=56 * 1024 * 1024),
        cost_estimate=pl.CostEstimate(
            flops=pairs * 30 * TILE * TILE * HD,
            bytes_accessed=30 * rows * width,
            transcendentals=pairs * TILE * TILE,
        ),
    )(idx, cnt, queries, grads, keys, values, low, high, *before)
    return out, dq, rest


def finish_kernel(own_tiles, k_own, v_own, ka, va, kb, vb, *refs):
    dk_ref, dv_ref = refs[-2:]
    a = pl.program_id(0)
    above = jnp.where(a >= own_tiles - SPT, 1.0, 0.0)
    below = jnp.where(a < SPT, 1.0, 0.0)
    for own, hi, lo, out in ((k_own, ka, kb, dk_ref), (v_own, va, vb, dv_ref)):
        total = own[0] + above * hi[0].astype(jnp.float32) + below * lo[0].astype(jnp.float32)
        out[...] = total.astype(jnp.bfloat16)


def finish(span, all_cols, dk_own, dv_own, from_above, from_below, before):
    own_tiles = dk_own.shape[0]
    width = span[1] * HD
    col_block = span[0] // span[1]
    own = pl.BlockSpec((1, TILE, width), lambda a: (a, 0, 0))

    def rim(shift, part):
        return pl.BlockSpec(
            (1, TILE, width), lambda a: (jnp.clip(a - shift, 0, SPT - 1), 0, part))

    out = pl.BlockSpec((TILE, width), lambda a: (a, col_block))
    shape = jax.ShapeDtypeStruct((own_tiles * TILE, all_cols), jnp.bfloat16)
    gap = own_tiles - SPT
    return pl.pallas_call(
        functools.partial(finish_kernel, own_tiles),
        grid=(own_tiles,),
        in_specs=[own, own, rim(gap, 0), rim(gap, 1), rim(0, 0), rim(0, 1)]
        + [pl.BlockSpec(memory_space=pl.ANY)] * len(before),
        out_specs=[out, out],
        out_shape=[shape, shape],
        input_output_aliases={6 + n: n for n in range(len(before))},
        compiler_params=pltpu.CompilerParams(vmem_limit_bytes=32 * 1024 * 1024),
        cost_estimate=pl.CostEstimate(
            flops=4 * own_tiles * TILE * width,
            bytes_accessed=20 * own_tiles * TILE * width,
            transcendentals=0,
        ),
    )(dk_own, dv_own, from_above, from_above, from_below, from_below, *before)


def neighbours(axis):
    count = lax.axis_size(axis)
    up = [(i, i + 1) for i in range(count - 1)]
    return up, [(b, a) for a, b in up]


def swap_blocks(blocks):
    return lax.all_to_all(blocks, "head", split_axis=0, concat_axis=0, tiled=True)


def head_plan(heads_here):
    size = 2
    groups = [(at, min(size, heads_here - at)) for at in range(0, heads_here, size)]
    first, last = groups[0], groups[-1]
    in_spans, out_spans = [first], [(0, last[0]), last]
    if heads_here > first[1]:
        in_spans.append((first[1], heads_here - first[1]))
    else:
        out_spans = [last]
    return groups, in_spans, out_spans


def span_of(head, spans):
    return [n for n, (at, count) in enumerate(spans) if at <= head < at + count][0]


def shards(queries, key_states, value_states, out_grads, pattern):
    row_count, col_count = queries.shape
    own_tiles = row_count // TILE
    head_devices = lax.axis_size("head")
    own_rows = out_grads.shape[0]
    first_tile = lax.axis_index("ctx") * own_tiles
    listed = lax.dynamic_slice_in_dim(pattern, first_tile, own_tiles, 0)
    allowed = listed >= 0
    idx = jnp.where(allowed, listed - (first_tile - SPT), 0).reshape(-1).astype(jnp.int32)
    cnt = jnp.sum(allowed.astype(jnp.int32), axis=1)
    up, down = neighbours("ctx")
    groups, in_spans, out_spans = head_plan(col_count // HD)
    keys_tiled = key_states.reshape(own_tiles, TILE, col_count)
    values_tiled = value_states.reshape(own_tiles, TILE, col_count)

    lows, highs, grads = [], [], []
    for at, heads in in_spans:
        cols = slice(at * HD, (at + heads) * HD)
        packed = jnp.concatenate((keys_tiled[:, :, cols], values_tiled[:, :, cols]), axis=2)
        grad_part = jnp.stack([
            out_grads[:, n * col_count + at * HD:n * col_count + (at + heads) * HD]
            for n in range(head_devices)
        ])
        if lows:
            packed, grad_part, lows[-1], highs[-1], grads[-1] = lax.optimization_barrier(
                (packed, grad_part, lows[-1], highs[-1], grads[-1]))
        lows.append(lax.ppermute(packed[own_tiles - SPT:], "ctx", up))
        highs.append(lax.ppermute(packed[:SPT], "ctx", down))
        grads.append(swap_blocks(grad_part).reshape(row_count, heads * HD))

    dq, parts, attended = None, [None] * len(out_spans), []
    for at, heads in groups:
        source, target = span_of(at, in_spans), span_of(at, out_spans)
        out, dq, parts[target] = attention(
            heads, at, in_spans[source], out_spans[target], idx, cnt, queries, grads[source],
            keys_tiled, values_tiled, lows[source], highs[source], dq, parts[target],
        )
        attended.append(swap_blocks(out.reshape(head_devices, own_rows, heads * HD)))

    sums = ()
    for span, (dk_own, dv_own, low, high) in zip(out_spans, parts):
        from_above = lax.ppermute(low, "ctx", down)
        from_below = lax.ppermute(high, "ctx", up)
        sums = finish(span, col_count, dk_own, dv_own, from_above, from_below, sums)
    attended = jnp.concatenate(
        [part[n] for n in range(head_devices) for part in attended], axis=1)
    return attended, dq, sums[0], sums[1]


def solution(mesh):
    return jax.shard_map(
        shards,
        mesh=mesh,
        in_specs=(
            P("ctx", "head"),
            P("ctx", "head"),
            P("ctx", "head"),
            P(("ctx", "head"), None),
            P(),
        ),
        out_specs=(P(("ctx", "head"), None), P("ctx", "head"), P("ctx", "head"), P("ctx", "head")),
        check_vma=False,
    )
```
